32 devices in a mesh: grp: 2 (over x), tp: 16 (over z, y, core).
Axes of the slice: x: 2, y: 2, z: 4, core: 2. Of those that a mesh axis runs over, the one named last changes fastest.
Arguments:
- queries: bfloat16 [256, 128, 576], P(('grp', 'tp'))
- kv_cache: bfloat16 [256, 512, 576], P(('grp', 'tp'))
- lengths: int32 [256], P(('grp', 'tp')), may hold values from 1 to 512, as said below
- residual: bfloat16 [256, 7168], P(('grp', 'tp')), may hold values from -6 to 6
- uv_weight: bfloat16 [128, 512, 128], P('tp'), may hold values from -1 to 1
- out_weight: bfloat16 [16384, 7168], P('tp'), may hold values from -0.1875 to 0.1875
- expert_ids: int32 [256, 8], P(('grp', 'tp')), may hold values from 0 to 15, all different within a row; in each aligned block of 8 rows (0 to 7, 8 to 15, ...) at most 8 rows name the same one
- gate_values: bfloat16 [256, 8], P(('grp', 'tp')), may hold values from 0.099609375 to 0.59765625
- w_gate: bfloat16 [16, 7168, 512], P('tp', None, 'grp'), may hold values from -0.0625 to 0.0625
- w_up: bfloat16 [16, 7168, 512], P('tp', None, 'grp'), may hold values from -0.0625 to 0.0625
- w_down: bfloat16 [16, 512, 7168], P('tp', 'grp'), may hold values from -0.25 to 0.25
Outputs:
- mixed: bfloat16 [256, 7168], P(('grp', 'tp'))
The draws below stay inside these ranges and needn't reach their ends.
Inputs may be any that keep to these rules, and one draw needn't show every extreme that they name: `lengths`: every row has at least one live position; in every draw some row has all 512 live. `expert_ids`: A row's 8 experts are distinct. Among the 8 rows of one device no expert is chosen more than 8 times, and in every draw some device reaches that count.
All inputs are finite; a program needn't handle non-finite values.
Results may differ from the reference program's by a relative error of at most 0.015.
Values may be sent and summed in bfloat16 or wider, within the bound.
A program may use at most 128 MiB of HBM per device.

```python
import math
import jax
import jax.numpy as jnp
import numpy as np
from jax import lax

D = 7168
HEADS = 128
KV_RANK = 512
ROPE = 64
VDIM = 128
TOPK = 8
ROWS_DEV = 8
CACHE_LEN = 512
EXPERT_FF = 512
EXPERTS = 16
CAP = 8
ROWS = 256
DEVICES = 32


def cache_values(key):
    return jax.random.normal(jax.random.fold_in(key, 11), (ROWS, CACHE_LEN, KV_RANK + ROPE), jnp.float32)


def draw_kv_cache(key, part):
    return cache_values(key).astype(jnp.bfloat16)


def draw_queries(key, part):
    key = jax.random.fold_in(key, 5)
    entries = jax.random.normal(key, (ROWS, HEADS, KV_RANK + ROPE), jnp.float32)
    return entries.astype(jnp.bfloat16)


def draw_lengths(key, part):
    key = jax.random.fold_in(key, 7)
    first, second = jax.random.split(key)
    drawn = jax.random.randint(first, (ROWS,), 1, CACHE_LEN + 1, dtype=jnp.int32)
    where_full = jax.random.randint(second, (), 0, ROWS, dtype=jnp.int32)
    return drawn.at[where_full].set(CACHE_LEN)


def steps_of(own_key, extent, cuts, low, high):
    def one(axis_at, shards_of):
        steps = jax.random.uniform(jax.random.fold_in(jax.random.fold_in(own_key, 6), axis_at), (shards_of,), jnp.float32, low / len(cuts), high / len(cuts))
        return jnp.repeat(jnp.exp(steps), extent[axis_at] // shards_of).reshape((-1,) + (1,) * (len(extent) - axis_at - 1))

    gain = one(*cuts[0])
    for cut in cuts[1:]:
        gain = gain * one(*cut)
    return gain


def shared_out(own_key, own, number, rows, amount, top, reach, slope):
    ranking = jax.random.permutation(own_key, amount)
    heavy_load, usual = shares(amount, rows * top, reach, slope, True), shares(amount, rows * top, reach, slope, False)
    places = jnp.arange(amount)

    def named(sizes, offset_by):
        used = int((sizes > 0).sum())
        fixed = max(1, used // 4)
        moved = fixed + (places - fixed + offset_by * (used - fixed)) % max(1, amount - fixed)
        return jnp.zeros((amount,), jnp.int32).at[ranking[jnp.where(places < fixed, places, moved)]].set(jnp.asarray(sizes, jnp.int32))

    sizes = jnp.where(number % 4 == 0, named(heavy_load, number // 4), named(usual, number - number // 4 - 1))
    mixed = jax.random.permutation(jax.random.fold_in(own, 3), amount)
    giver, receiver = mixed[0:amount // 2 * 2:2], mixed[1:amount // 2 * 2:2]
    slack = jnp.minimum(sizes[giver] - 1, reach - sizes[receiver]) // 2
    slack = jnp.where((giver == ranking[0]) | (receiver == ranking[0]) | (sizes[receiver] == 0), 0, jnp.maximum(slack, 0))
    moved = jax.random.randint(jax.random.fold_in(own, 4), (amount // 2,), 0, 1 << 20) % (slack + 1)
    sizes = sizes.at[giver].add(-moved).at[receiver].add(moved)
    members = jnp.searchsorted(jnp.cumsum(sizes), jnp.arange(rows * top), side="right").astype(jnp.int32)
    table = members.reshape(top, rows).T
    table = table[jax.random.permutation(jax.random.fold_in(own, 1), rows)]
    offset_by = jax.random.randint(jax.random.fold_in(own, 2), (rows, 1), 0, top)
    return jnp.take_along_axis(table, (jnp.arange(top)[None, :] + offset_by) % top, axis=1)


def shares(number_of, total, most, slope, full):
    portions = [(1 << 20) // math.isqrt(standing ** slope) + 1 for standing in range(1, number_of + 1)]
    largest = most if full else min(most, max(-(-total // number_of), total * portions[0] // sum(portions)))
    least = 1 if total - largest >= number_of - 1 else 0
    given, surplus = [largest] + [least] * (number_of - 1), total - largest - least * (number_of - 1)
    while surplus > 0:
        free = [i for i in range(1, number_of) if given[i] < largest] or [i for i in range(1, number_of) if given[i] < most]
        mass, budget = sum([portions[i] for i in free]), surplus
        for i in free:
            addition = min(most - given[i], max(1, budget * portions[i] // mass), surplus)
            given[i] = given[i] + addition
            surplus = surplus - addition
    return np.array(given)


def bell_draw(stream_key, extent, spread, reach, shards=(), kind=jnp.bfloat16):
    values = spread * jax.random.normal(stream_key, extent, jnp.float32)
    if shards:
        values = values * steps_of(stream_key, extent, shards, -0.22, 0.18)
    return jnp.clip(values, -reach, reach).astype(kind)


def setup_inputs(seed: int = 0) -> dict:
    key_list = jax.random.split(jax.random.key(seed), 12)
    queries = draw_queries(jax.random.fold_in(key_list[11], 71), 0)
    kv_cache = draw_kv_cache(jax.random.fold_in(key_list[11], 71), 0)
    lengths = draw_lengths(jax.random.fold_in(key_list[11], 71), 0)
    residual = bell_draw(key_list[3], (ROWS, D), 1.0, 6.0, ((0, 32),))
    uv_weight = bell_draw(key_list[4], (HEADS, KV_RANK, VDIM), (KV_RANK // 16) ** -0.5, 1.0, ((0, 16),))
    out_weight = bell_draw(key_list[5], (HEADS * VDIM, D), (HEADS * VDIM // 16) ** -0.5, 0.1875, ((0, 16),))
    expert_ids_keys = jax.random.split(jax.random.fold_in(key_list[6], 1), ROWS // ROWS_DEV)
    expert_ids_turns = jax.random.permutation(jax.random.fold_in(key_list[6], 3), ROWS // ROWS_DEV)
    expert_ids = jax.vmap(lambda own, number: shared_out(jax.random.fold_in(key_list[6], 2), own, number, ROWS_DEV, EXPERTS, TOPK, CAP, 2))(expert_ids_keys, expert_ids_turns).reshape((ROWS, TOPK))
    gate_values = jnp.clip(0.099609375 + 0.49804688 * jax.random.uniform(key_list[7], (ROWS, TOPK), jnp.float32) ** steps_of(key_list[7], (ROWS, TOPK), ((0, 32),), -0.2, 0.2), 0.099609375, 0.59765625).astype(jnp.bfloat16)
    w_gate = bell_draw(key_list[8], (EXPERTS, D, EXPERT_FF), D ** -0.5, 0.0625, ((0, 16), (2, 2)))
    w_up = bell_draw(key_list[9], (EXPERTS, D, EXPERT_FF), D ** -0.5, 0.0625, ((0, 16), (2, 2)))
    w_down = bell_draw(key_list[10], (EXPERTS, EXPERT_FF, D), EXPERT_FF ** -0.5, 0.25, ((0, 16), (1, 2)))
    return dict(queries=queries, kv_cache=kv_cache, lengths=lengths, residual=residual, uv_weight=uv_weight, out_weight=out_weight, expert_ids=expert_ids, gate_values=gate_values, w_gate=w_gate, w_up=w_up, w_down=w_down)


def attend(item):
    query, cache, live = item
    scores = jnp.einsum('rhc,rlc->rhl', query.astype(jnp.float32), cache.astype(jnp.float32)) * (KV_RANK + ROPE) ** (-0.5)
    valid = lax.broadcasted_iota(jnp.int32, (1, 1, CACHE_LEN), 2) < live.astype(jnp.int32)[:, None, None]
    top = lax.optimization_barrier(jnp.max(jnp.where(valid, scores, -jnp.inf), axis=-1, keepdims=True))
    expo = jnp.where(valid, jnp.exp(scores - top), 0.0)
    probs = (expo / lax.optimization_barrier(jnp.sum(expo, axis=-1, keepdims=True))).astype(jnp.bfloat16)
    context = jnp.einsum('rhl,rlc->rhc', probs.astype(jnp.float32), cache[:, :, :KV_RANK].astype(jnp.float32))
    return context.astype(jnp.bfloat16)

def reference(queries, kv_cache, lengths, residual, uv_weight, out_weight, expert_ids, gate_values, w_gate, w_up, w_down):
    blocks = ROWS // ROWS_DEV
    context = lax.map(attend, (queries.reshape(blocks, ROWS_DEV, HEADS, KV_RANK + ROPE), kv_cache.reshape(blocks, ROWS_DEV, CACHE_LEN, KV_RANK + ROPE), lengths.reshape(blocks, ROWS_DEV)))
    context = context.reshape(ROWS, HEADS, KV_RANK)
    values = jnp.einsum('rhc,hcv->rhv', context.astype(jnp.float32), uv_weight.astype(jnp.float32))
    values = values.astype(jnp.bfloat16).reshape(ROWS, HEADS * VDIM)
    hidden_state = residual.astype(jnp.float32) + jnp.dot(values, out_weight, preferred_element_type=jnp.float32)
    normed = (hidden_state * lax.rsqrt(lax.optimization_barrier(jnp.mean(hidden_state * hidden_state, axis=-1, keepdims=True)) + 1e-06)).astype(jnp.bfloat16)
    flat = expert_ids.reshape(-1).astype(jnp.int32)
    weight_flat = gate_values.reshape(-1).astype(jnp.float32)
    most_rows = min(CAP * DEVICES, ROWS * TOPK)

    def one_expert(carry, item):
        number, gate_mat, up_mat, down_mat = item
        keyed = jnp.where(flat == number, 0, 1).astype(jnp.int32)
        order = jnp.argsort(keyed, stable=True)[:most_rows].astype(jnp.int32)
        picked = (order // TOPK).astype(jnp.int32)
        weight = jnp.where(flat[order] == number, weight_flat[order], 0.0)
        taken = normed[picked]
        gate = jnp.dot(taken, gate_mat, preferred_element_type=jnp.float32)
        up = jnp.dot(taken, up_mat, preferred_element_type=jnp.float32)
        hidden = (jax.nn.silu(gate) * up).astype(jnp.bfloat16)
        output = jnp.dot(hidden, down_mat, preferred_element_type=jnp.float32) * weight[:, None]
        return (carry.at[picked].add(output), None)
    routed, _ = lax.scan(one_expert, jnp.zeros((ROWS, D), jnp.float32), (jnp.arange(EXPERTS, dtype=jnp.int32), w_gate, w_up, w_down))
    return (hidden_state + routed).astype(jnp.bfloat16)
```

```python
import jax
import jax.numpy as jnp
from jax import lax
from jax.sharding import PartitionSpec as P


def body(
    queries,
    kv_cache,
    lengths,
    residual,
    uv_weight,
    out_weight,
    expert_ids,
    gate_values,
    w_gate,
    w_up,
    w_down,
):
    rows_here = residual.shape[0]
    latent = uv_weight.shape[1]
    width = residual.shape[1]
    span = kv_cache.shape[1]
    scores = jnp.einsum(
        "rhc,rlc->rhl", queries, kv_cache, preferred_element_type=jnp.float32
    ) * queries.shape[2] ** (-0.5)
    valid = lax.broadcasted_iota(jnp.int32, (1, 1, span), 2) < lengths[:, None, None]
    top = jnp.max(jnp.where(valid, scores, -jnp.inf), axis=-1, keepdims=True)
    expo = jnp.where(valid, jnp.exp(scores - top), 0.0)
    probs = (expo / jnp.sum(expo, axis=-1, keepdims=True)).astype(jnp.bfloat16)
    context = jnp.einsum(
        "rhl,rlc->rhc", probs, kv_cache[:, :, :latent], preferred_element_type=jnp.float32
    ).astype(jnp.bfloat16)
    grouped = lax.all_to_all(context, "tp", split_axis=1, concat_axis=0, tiled=True)
    values = jnp.einsum(
        "rhc,hcv->rhv", grouped, uv_weight, preferred_element_type=jnp.float32
    ).astype(jnp.bfloat16)
    values = values.reshape(values.shape[0], values.shape[1] * values.shape[2])
    attention = lax.psum_scatter(
        jnp.dot(values, out_weight, preferred_element_type=jnp.float32).astype(jnp.bfloat16),
        "tp",
        scatter_dimension=0,
        tiled=True,
    ).astype(jnp.float32)
    hidden_state = residual.astype(jnp.float32) + attention
    normed = (
        hidden_state
        * lax.rsqrt(jnp.mean(hidden_state * hidden_state, axis=-1, keepdims=True) + 1e-06)
    ).astype(jnp.bfloat16)
    experts = lax.axis_size("tp")
    me = lax.axis_index("tp")
    ids_hot = expert_ids[:, :, None] == lax.broadcasted_iota(jnp.int32, (1, 1, experts), 2)
    weights = jnp.sum(
        jnp.where(ids_hot, gate_values.astype(jnp.float32)[:, :, None], 0.0), axis=1
    ).astype(jnp.bfloat16)
    weights_all = lax.all_gather(weights, ("grp", "tp"), axis=0, tiled=True)
    own = lax.broadcasted_iota(jnp.int32, (1, experts), 1) == me
    weight = jnp.sum(
        jnp.where(own, weights_all.astype(jnp.float32), 0.0), axis=1, keepdims=True
    )
    rows_all = lax.all_gather(normed, ("grp", "tp"), axis=0, tiled=True)
    gate = jnp.dot(rows_all, w_gate[0], preferred_element_type=jnp.float32)
    up = jnp.dot(rows_all, w_up[0], preferred_element_type=jnp.float32)
    hidden = (jax.nn.silu(gate) * up * weight).astype(jnp.bfloat16)
    partial_value = jnp.dot(hidden, w_down[0], preferred_element_type=jnp.float32)
    routed = lax.psum_scatter(
        partial_value.astype(jnp.bfloat16), ("grp", "tp"), scatter_dimension=0, tiled=True
    ).astype(jnp.float32)
    return (hidden_state + routed).astype(jnp.bfloat16)


def solution(mesh):
    placed = (
        P(("grp", "tp"), None, None),
        P(("grp", "tp"), None, None),
        P(("grp", "tp")),
        P(("grp", "tp"), None),
        P("tp", None, None),
        P("tp", None),
        P(("grp", "tp"), None),
        P(("grp", "tp"), None),
        P("tp", None, "grp"),
        P("tp", None, "grp"),
        P("tp", "grp", None),
    )
    return jax.shard_map(
        body, mesh=mesh, in_specs=placed, out_specs=P(("grp", "tp"), None), check_vma=False
    )
```

```python
import functools
import jax
import jax.numpy as jnp
from jax import lax
from jax.experimental import pallas as pl
from jax.experimental.pallas import tpu as pltpu
from jax.sharding import PartitionSpec as P

MESH = pl.DeviceIdType.MESH
F32, BF16 = jnp.float32, jnp.bfloat16


def axis_bits(groups, peers):
    grp = [("grp", 1, False)] if groups == 2 else [("grp", 2, True), ("grp", 1, False)]
    tp = [("tp", peers // 2, True), ("tp", peers // 4, False)]
    tp += [("tp", 2, False)] if peers // 8 == 2 else [("tp", 4, True), ("tp", 2, False)]
    return grp, tp


def chain_orders(bits):
    near = [i for i, b in enumerate(bits) if not b[2]]
    far = [i for i, b in enumerate(bits) if b[2]]
    turn = lambda xs, k: xs[k % len(xs):] + xs[: k % len(xs)] if xs else []
    return [turn(near, k) + turn(far, k) for k in range(len(near))]


def column_parts(half, n):
    tiles = half // 128
    cuts = [128 * (tiles * k // n) for k in range(n + 1)]
    return [(cuts[k], cuts[k + 1] - cuts[k]) for k in range(n)]


class Place:
    def __init__(self, bits):
        self.g, self.t = lax.axis_index("grp"), lax.axis_index("tp")
        self.core = self.t % 2
        self.sibling = (self.g, self.t + 1 - 2 * self.core)
        self.mine, self.partner = [], []
        for axis, value, _ in bits:
            at = self.g if axis == "grp" else self.t
            bit = (at // value) % 2
            moved = at + value * (1 - 2 * bit)
            self.mine.append(bit)
            self.partner.append((moved, self.t) if axis == "grp" else (self.g, moved))

    def greet(self):
        barrier = pltpu.get_barrier_semaphore()
        others = [self.sibling] + self.partner
        for other in others:
            pl.semaphore_signal(barrier, inc=1, device_id=other, device_id_type=MESH)
        pl.semaphore_wait(barrier, len(others))


def send(src, dst, sems, at, to):
    copy = pltpu.make_async_remote_copy(
        src_ref=src,
        dst_ref=dst,
        send_sem=sems[0].at[at],
        recv_sem=sems[1].at[at],
        device_id=to,
        device_id_type=MESH,
    )
    copy.start()
    return copy


def columns(start, size):
    return pl.ds(pl.multiple_of(start, 128), size)


def scatter_scratch(bits, half):
    shapes = [pltpu.VMEM((2,) * len(bits) + (16, half), BF16), pltpu.VMEM((2, 8, half), F32)]
    shapes += [pltpu.VMEM((8, half), F32)]
    orders = chain_orders(bits)
    for _, width in column_parts(half, len(orders)):
        for done in range(len(bits) + 1):
            shapes.append(pltpu.VMEM((2,) * (len(bits) - done) + (16, width), BF16))
    count = len(orders) * (len(bits) + 2)
    return shapes + [pltpu.SemaphoreType.DMA((count,)), pltpu.SemaphoreType.DMA((count,))]


def reduce_scatter(bits, place, half, x_ref, out_ref, scratch):
    held, own, swapped = scratch[:3]
    sems = scratch[-2:]
    orders = chain_orders(bits)
    parts = column_parts(half, len(orders))
    n = len(bits)
    landed = [scratch[3 + k * (n + 1): 3 + (k + 1) * (n + 1)] for k in range(len(orders))]
    every = (slice(None),) * (n + 1)
    core = place.core
    copies, now = [], []

    def launch(*what):
        copy = send(*what)
        copies.append(copy)
        return copy

    for k, (start, width) in enumerate(parts):
        src = x_ref.at[every + (columns((1 - core) * half + start, width),)]
        now.append(launch(src, landed[k][0], sems, k * (n + 2), place.sibling))
    for stage in range(n + 1):
        for k, (start, width) in enumerate(parts):
            here = pl.ds(start, width)
            now[k].wait_recv()
            done = orders[k][:stage]
            keep = tuple(place.mine[i] if i in done else slice(None) for i in range(n)) + (slice(None),)
            base = (
                x_ref[every + (columns(core * half + start, width),)]
                if stage == 0
                else held[keep + (here,)]
            )
            total = base.astype(F32) + landed[k][stage][...].astype(F32)
            if stage < n:
                held[keep + (here,)] = total.astype(BF16)
                bit = orders[k][stage]
                away = tuple(
                    1 - place.mine[i] if i == bit else keep[i] for i in range(n)
                ) + (slice(None), here)
                now[k] = launch(
                    held.at[away], landed[k][stage + 1], sems, k * (n + 2) + stage + 1, place.partner[bit]
                )
            else:
                own[0, :, here] = total[:8]
                own[1, :, here] = total[8:]
                now[k] = launch(
                    own.at[1 - core, :, here], swapped.at[:, here], sems, k * (n + 2) + n + 1, place.sibling
                )
    for k, (start, width) in enumerate(parts):
        here = pl.ds(start, width)
        out_ref[:, columns(core * half + start, width)] = own[core, :, here]
        now[k].wait_recv()
        out_ref[:, columns((1 - core) * half + start, width)] = swapped[:, here]
    for copy in copies:
        copy.wait_send()


def gather_scratch(bits, half):
    orders = chain_orders(bits)
    count = len(orders) * (len(bits) + 2)
    return [
        pltpu.VMEM((8, half), F32),
        pltpu.SemaphoreType.DMA((count,)),
        pltpu.SemaphoreType.DMA((count,)),
    ]


def gather(bits, place, half, rows_ref, out_ref, scratch):
    swapped, sems = scratch[0], scratch[1:]
    orders = chain_orders(bits)
    parts = column_parts(half, len(orders))
    n = len(bits)
    core = place.core
    copies, now = [], []

    def launch(*what):
        copy = send(*what)
        copies.append(copy)
        return copy

    for k, (start, width) in enumerate(parts):
        src = rows_ref.at[:, columns((1 - core) * half + start, width)]
        now.append(launch(src, swapped.at[:, pl.ds(start, width)], sems, k * (n + 2), place.sibling))
    for stage in range(n + 1):
        for k, (start, width) in enumerate(parts):
            here = columns(core * half + start, width)
            now[k].wait_recv()
            order = orders[k][::-1]
            if stage == 0:
                mine, other = rows_ref[:, here], swapped[:, pl.ds(start, width)]
                first = jnp.where(core == 0, mine, other)
                second = jnp.where(core == 0, other, mine)
                block = jnp.concatenate([first, second], axis=0).astype(BF16)
                out_ref[tuple(place.mine) + (slice(None), here)] = block
            done = order[:stage]
            at = tuple(slice(None) if i in done else place.mine[i] for i in range(n))
            part = out_ref.at[at + (slice(None), here)]
            to = place.partner[order[stage]] if stage < n else place.sibling
            now[k] = launch(part, part, sems, k * (n + 2) + stage + 1, to)
    for k in range(len(parts)):
        now[k].wait_recv()
    for copy in copies:
        copy.wait_send()


def middle_kernel(tp_bits, all_bits, x_ref, residual_ref, hidden_ref, rows_ref, normed, *scratch):
    half = residual_ref.shape[1] // 2
    place_all = Place(all_bits)
    place = Place(tp_bits)
    place_all.greet()
    cut = len(scatter_scratch(tp_bits, half))
    reduce_scatter(tp_bits, place, half, x_ref, hidden_ref, scratch[:cut])
    state = hidden_ref[...] + residual_ref[...].astype(F32)
    hidden_ref[...] = state
    normed[...] = state * lax.rsqrt(jnp.mean(state * state, axis=-1, keepdims=True) + 1e-06)
    gather(all_bits, place_all, half, normed, rows_ref, scratch[cut:])


def final_kernel(all_bits, x_ref, hidden_ref, out_ref, routed, *scratch):
    half = hidden_ref.shape[1] // 2
    place = Place(all_bits)
    place.greet()
    reduce_scatter(all_bits, place, half, x_ref, routed, scratch)
    out_ref[...] = (routed[...] + hidden_ref[...]).astype(out_ref.dtype)


VMEM = pl.BlockSpec(memory_space=pltpu.VMEM)


def middle(part, residual, groups, peers):
    width = residual.shape[1]
    grp_bits, tp_bits = axis_bits(groups, peers)
    both = grp_bits + tp_bits
    rows = groups * peers * 8
    need = width * 2 * (3 * part.shape[0] + rows) + (12 << 20)
    hidden, gathered = pl.pallas_call(
        functools.partial(middle_kernel, tp_bits, both),
        out_shape=(
            jax.ShapeDtypeStruct((8, width), F32),
            jax.ShapeDtypeStruct((2,) * len(both) + (16, width), BF16),
        ),
        in_specs=[VMEM, VMEM],
        out_specs=(VMEM, VMEM),
        scratch_shapes=[pltpu.VMEM((8, width), F32)]
        + scatter_scratch(tp_bits, width // 2)
        + gather_scratch(both, width // 2),
        compiler_params=pltpu.CompilerParams(
            collective_id=0, has_side_effects=True, vmem_limit_bytes=need
        ),
    )(part.reshape((2,) * len(tp_bits) + (16, width)), residual)
    return hidden, gathered.reshape(rows, width)


def final(part, hidden, groups, peers):
    width = hidden.shape[1]
    grp_bits, tp_bits = axis_bits(groups, peers)
    both = grp_bits + tp_bits
    need = width * 2 * 3 * part.shape[0] + (12 << 20)
    return pl.pallas_call(
        functools.partial(final_kernel, both),
        out_shape=jax.ShapeDtypeStruct((8, width), BF16),
        in_specs=[VMEM, VMEM],
        out_specs=VMEM,
        scratch_shapes=[pltpu.VMEM((8, width), F32)] + scatter_scratch(both, width // 2),
        compiler_params=pltpu.CompilerParams(
            collective_id=1, has_side_effects=True, vmem_limit_bytes=need
        ),
    )(part.reshape((2,) * len(both) + (16, width)), hidden)


def body(
    queries,
    kv_cache,
    lengths,
    residual,
    uv_weight,
    out_weight,
    expert_ids,
    gate_values,
    w_gate,
    w_up,
    w_down,
):
    rows_here = residual.shape[0]
    latent = uv_weight.shape[1]
    width = residual.shape[1]
    span = kv_cache.shape[1]
    scores = jnp.einsum(
        "rhc,rlc->rhl", queries, kv_cache, preferred_element_type=jnp.float32
    ) * queries.shape[2] ** (-0.5)
    valid = lax.broadcasted_iota(jnp.int32, (1, 1, span), 2) < lengths[:, None, None]
    top = jnp.max(jnp.where(valid, scores, -jnp.inf), axis=-1, keepdims=True)
    expo = jnp.where(valid, jnp.exp(scores - top), 0.0)
    probs = (expo / jnp.sum(expo, axis=-1, keepdims=True)).astype(jnp.bfloat16)
    context = jnp.einsum(
        "rhl,rlc->rhc", probs, kv_cache[:, :, :latent], preferred_element_type=jnp.float32
    ).astype(jnp.bfloat16)
    grouped = lax.all_to_all(context, "tp", split_axis=1, concat_axis=0, tiled=True)
    values = jnp.einsum(
        "rhc,hcv->rhv", grouped, uv_weight, preferred_element_type=jnp.float32
    ).astype(jnp.bfloat16)
    values = values.reshape(values.shape[0], values.shape[1] * values.shape[2])
    groups, peers = lax.axis_size("grp"), lax.axis_size("tp")
    attention = jnp.dot(values, out_weight, preferred_element_type=jnp.float32).astype(BF16)
    hidden_state, rows_all = middle(attention, residual, groups, peers)
    experts = lax.axis_size("tp")
    me = lax.axis_index("tp")
    ids_hot = expert_ids[:, :, None] == lax.broadcasted_iota(jnp.int32, (1, 1, experts), 2)
    weights = jnp.sum(
        jnp.where(ids_hot, gate_values.astype(jnp.float32)[:, :, None], 0.0), axis=1
    ).astype(jnp.bfloat16)
    weights_all = lax.all_gather(weights, ("grp", "tp"), axis=0, tiled=True)
    own = lax.broadcasted_iota(jnp.int32, (1, experts), 1) == me
    weight = jnp.sum(
        jnp.where(own, weights_all.astype(jnp.float32), 0.0), axis=1, keepdims=True
    )
    gate = jnp.dot(rows_all, w_gate[0], preferred_element_type=jnp.float32)
    up = jnp.dot(rows_all, w_up[0], preferred_element_type=jnp.float32)
    hidden = (jax.nn.silu(gate) * up * weight).astype(jnp.bfloat16)
    partial_value = jnp.dot(hidden, w_down[0], preferred_element_type=jnp.float32)
    return final(partial_value.astype(jnp.bfloat16), hidden_state, groups, peers)


def solution(mesh):
    placed = (
        P(("grp", "tp"), None, None),
        P(("grp", "tp"), None, None),
        P(("grp", "tp")),
        P(("grp", "tp"), None),
        P("tp", None, None),
        P("tp", None),
        P(("grp", "tp"), None),
        P(("grp", "tp"), None),
        P("tp", None, "grp"),
        P("tp", None, "grp"),
        P("tp", "grp", None),
    )
    return jax.shard_map(
        body, mesh=mesh, in_specs=placed, out_specs=P(("grp", "tp"), None), check_vma=False
    )
```

```python
import functools
import jax
import jax.numpy as jnp
from jax import lax
from jax.experimental import pallas as pl
from jax.experimental.pallas import tpu as pltpu
from jax.sharding import PartitionSpec as P

TILE = 256
MESH = pl.DeviceIdType.MESH
F32, BF16 = jnp.float32, jnp.bfloat16


def axis_bits(groups, peers):
    grp = [("grp", 1, False)] if groups == 2 else [("grp", 2, True), ("grp", 1, False)]
    tp = [("tp", peers // 2, True), ("tp", peers // 4, False)]
    tp += [("tp", 2, False)] if peers // 8 == 2 else [("tp", 4, True), ("tp", 2, False)]
    return grp, tp


def chain_orders(bits):
    near = [i for i, b in enumerate(bits) if not b[2]]
    far = [i for i, b in enumerate(bits) if b[2]]
    turn = lambda xs, k: xs[k % len(xs):] + xs[: k % len(xs)] if xs else []
    return [turn(near, k) + turn(far, k) for k in range(len(near))]


def column_parts(half, n):
    tiles = half // TILE
    cuts = [TILE * (tiles * k // n) for k in range(n + 1)]
    return [(cuts[k], cuts[k + 1] - cuts[k]) for k in range(n)]


class Place:
    def __init__(self, bits):
        self.g, self.t = lax.axis_index("grp"), lax.axis_index("tp")
        self.core = self.t % 2
        self.sibling = (self.g, self.t + 1 - 2 * self.core)
        self.mine, self.partner = [], []
        for axis, value, _ in bits:
            at = self.g if axis == "grp" else self.t
            bit = (at // value) % 2
            moved = at + value * (1 - 2 * bit)
            self.mine.append(bit)
            self.partner.append((moved, self.t) if axis == "grp" else (self.g, moved))

    def greet(self):
        barrier = pltpu.get_barrier_semaphore()
        others = [self.sibling] + self.partner
        for other in others:
            pl.semaphore_signal(barrier, inc=1, device_id=other, device_id_type=MESH)
        pl.semaphore_wait(barrier, len(others))


def send(src, dst, sems, at, to):
    copy = pltpu.make_async_remote_copy(
        src_ref=src,
        dst_ref=dst,
        send_sem=sems[0].at[at],
        recv_sem=sems[1].at[at],
        device_id=to,
        device_id_type=MESH,
    )
    copy.start()
    return copy


def columns(start, size):
    return pl.ds(pl.multiple_of(start, 128), size)


def scatter_scratch(bits, half):
    shapes = [pltpu.VMEM((2,) * len(bits) + (16, half), BF16), pltpu.VMEM((2, 8, half), F32)]
    shapes += [pltpu.VMEM((8, half), F32), pltpu.VMEM((2,) * len(bits) + (16, half), BF16)]
    orders = chain_orders(bits)
    for _, width in column_parts(half, len(orders)):
        for done in range(len(bits) + 1):
            shapes.append(pltpu.VMEM((2,) * (len(bits) - done) + (16, width), BF16))
    count = len(orders) * (len(bits) + 2)
    return shapes + [pltpu.SemaphoreType.DMA((count,)), pltpu.SemaphoreType.DMA((count,))]


def reduce_scatter(bits, place, half, left_ref, right_ref, out_ref, scratch):
    held, own, swapped, leaving = scratch[:4]
    sems = scratch[-2:]
    orders = chain_orders(bits)
    parts = column_parts(half, len(orders))
    n = len(bits)
    landed = [scratch[4 + k * (n + 1): 4 + (k + 1) * (n + 1)] for k in range(len(orders))]
    every = (slice(None),) * (n + 1)
    core = place.core
    copies, now = [], []

    def launch(*what):
        copy = send(*what)
        copies.append(copy)
        return copy

    def product(offset, start, width, store):
        def tile(i, carry):
            at = pl.multiple_of(start + i * TILE, TILE)
            right = right_ref[:, columns(offset + at, TILE)]
            value = jnp.dot(left_ref[...], right, preferred_element_type=F32)
            store(pl.ds(at, TILE), value)
            return carry

        lax.fori_loop(0, width // TILE, tile, 0)

    def leave(here, value):
        leaving[every + (here,)] = value.astype(BF16).reshape(leaving.shape[:-1] + (TILE,))

    def stay(here, value):
        held[every + (here,)] = value.astype(BF16).reshape(held.shape[:-1] + (TILE,))

    for k, (start, width) in enumerate(parts):
        product((1 - core) * half, start, width, leave)
        src = leaving.at[every + (pl.ds(start, width),)]
        now.append(launch(src, landed[k][0], sems, k * (n + 2), place.sibling))
    for start, width in parts:
        product(core * half, start, width, stay)
    for stage in range(n + 1):
        for k, (start, width) in enumerate(parts):
            here = pl.ds(start, width)
            now[k].wait_recv()
            done = orders[k][:stage]
            keep = tuple(place.mine[i] if i in done else slice(None) for i in range(n)) + (slice(None),)
            total = held[keep + (here,)].astype(F32) + landed[k][stage][...].astype(F32)
            if stage < n:
                held[keep + (here,)] = total.astype(BF16)
                bit = orders[k][stage]
                away = tuple(
                    1 - place.mine[i] if i == bit else keep[i] for i in range(n)
                ) + (slice(None), here)
                now[k] = launch(
                    held.at[away], landed[k][stage + 1], sems, k * (n + 2) + stage + 1, place.partner[bit]
                )
            else:
                own[0, :, here] = total[:8]
                own[1, :, here] = total[8:]
                now[k] = launch(
                    own.at[1 - core, :, here], swapped.at[:, here], sems, k * (n + 2) + n + 1, place.sibling
                )
    for k, (start, width) in enumerate(parts):
        here = pl.ds(start, width)
        out_ref[:, columns(core * half + start, width)] = own[core, :, here]
        now[k].wait_recv()
        out_ref[:, columns((1 - core) * half + start, width)] = swapped[:, here]
    for copy in copies:
        copy.wait_send()


def gather_scratch(bits, half):
    orders = chain_orders(bits)
    count = (len(orders) + 1) * (len(bits) + 2)
    return [
        pltpu.VMEM((8, half), F32),
        pltpu.VMEM((8, 128), F32),
        pltpu.SemaphoreType.DMA((count,)),
        pltpu.SemaphoreType.DMA((count,)),
    ]


def gather(bits, place, half, rows_ref, small_ref, out_ref, small_out, scratch):
    swapped, small_swapped, sems = scratch[0], scratch[1], scratch[2:]
    orders = chain_orders(bits)
    parts = column_parts(half, len(orders))
    n = len(bits)
    core = place.core
    copies, now = [], []

    def launch(*what):
        copy = send(*what)
        copies.append(copy)
        return copy

    for k, (start, width) in enumerate(parts):
        src = rows_ref.at[:, columns((1 - core) * half + start, width)]
        now.append(launch(src, swapped.at[:, pl.ds(start, width)], sems, k * (n + 2), place.sibling))
    now.append(launch(small_ref, small_swapped, sems, len(parts) * (n + 2), place.sibling))

    def chip_block(mine, other):
        first = jnp.where(core == 0, mine, other)
        second = jnp.where(core == 0, other, mine)
        return jnp.concatenate([first, second], axis=0).astype(BF16)

    own = tuple(place.mine) + (slice(None),)
    for stage in range(n + 1):
        k = len(parts)
        now[k].wait_recv()
        order = orders[0][::-1]
        if stage == 0:
            small_out[own + (slice(None),)] = chip_block(small_ref[...], small_swapped[...])
        if stage < n:
            done = order[:stage]
            at = tuple(slice(None) if i in done else place.mine[i] for i in range(n))
            part = small_out.at[at + (slice(None), slice(None))]
            now[k] = launch(part, part, sems, k * (n + 2) + stage + 1, place.partner[order[stage]])
        for k, (start, width) in enumerate(parts):
            here = columns(core * half + start, width)
            now[k].wait_recv()
            order = orders[k][::-1]
            if stage == 0:
                block = chip_block(rows_ref[:, here], swapped[:, pl.ds(start, width)])
                out_ref[own + (here,)] = block
            done = order[:stage]
            at = tuple(slice(None) if i in done else place.mine[i] for i in range(n))
            part = out_ref.at[at + (slice(None), here)]
            to = place.partner[order[stage]] if stage < n else place.sibling
            now[k] = launch(part, part, sems, k * (n + 2) + stage + 1, to)
    for k in range(len(parts)):
        now[k].wait_recv()
    for copy in copies:
        copy.wait_send()


def middle_kernel(
    tp_bits, all_bits, values_ref, out_weight_ref, residual_ref, weights_ref,
    hidden_ref, rows_ref, weights_out, normed, *scratch
):
    half = residual_ref.shape[1] // 2
    place_all = Place(all_bits)
    place = Place(tp_bits)
    place_all.greet()
    cut = len(scatter_scratch(tp_bits, half))
    reduce_scatter(tp_bits, place, half, values_ref, out_weight_ref, hidden_ref, scratch[:cut])
    state = hidden_ref[...] + residual_ref[...].astype(F32)
    hidden_ref[...] = state
    normed[...] = state * lax.rsqrt(jnp.mean(state * state, axis=-1, keepdims=True) + 1e-06)
    gather(all_bits, place_all, half, normed, weights_ref, rows_ref, weights_out, scratch[cut:])


def final_kernel(all_bits, inner_ref, w_down_ref, hidden_ref, out_ref, routed, *scratch):
    half = hidden_ref.shape[1] // 2
    place = Place(all_bits)
    place.greet()
    reduce_scatter(all_bits, place, half, inner_ref, w_down_ref, routed, scratch)
    out_ref[...] = (routed[...] + hidden_ref[...]).astype(out_ref.dtype)


def exchange_kernel(peers, x_ref, out_ref, send_sems, recv_sems, own_sem):
    g, t = lax.axis_index("grp"), lax.axis_index("tp")
    shifts = sorted(range(1, peers), key=lambda d: (abs(d - peers // 2), d))
    barrier = pltpu.get_barrier_semaphore()
    for d in shifts:
        pl.semaphore_signal(
            barrier, inc=1, device_id=(g, (t + d) % peers), device_id_type=MESH
        )
    pl.semaphore_wait(barrier, peers - 1)
    copies = []
    for d in shifts:
        to = (t + d) % peers
        copies.append(send(x_ref.at[to], out_ref.at[t], (send_sems, recv_sems), d, (g, to)))
    own = pltpu.make_async_copy(x_ref.at[t], out_ref.at[t], own_sem)
    own.start()
    own.wait()
    for copy in copies:
        copy.wait_recv()
    for copy in copies:
        copy.wait_send()


VMEM = pl.BlockSpec(memory_space=pltpu.VMEM)


def exchange(blocks, peers):
    return pl.pallas_call(
        functools.partial(exchange_kernel, peers),
        out_shape=jax.ShapeDtypeStruct(blocks.shape, blocks.dtype),
        in_specs=[VMEM],
        out_specs=VMEM,
        scratch_shapes=[
            pltpu.SemaphoreType.DMA((peers,)),
            pltpu.SemaphoreType.DMA((peers,)),
            pltpu.SemaphoreType.DMA(()),
        ],
        compiler_params=pltpu.CompilerParams(
            collective_id=2, has_side_effects=True, vmem_limit_bytes=8 << 20
        ),
    )(blocks)


def middle(values, out_weight, residual, weights, groups, peers):
    width = residual.shape[1]
    grp_bits, tp_bits = axis_bits(groups, peers)
    both = grp_bits + tp_bits
    rows = groups * peers * 8
    need = width * 2 * (3 * values.shape[0] + rows + values.shape[1]) + (12 << 20)
    shape = (2,) * len(both) + (16,)
    hidden, gathered, weights_all = pl.pallas_call(
        functools.partial(middle_kernel, tp_bits, both),
        out_shape=(
            jax.ShapeDtypeStruct((8, width), F32),
            jax.ShapeDtypeStruct(shape + (width,), BF16),
            jax.ShapeDtypeStruct(shape + (128,), BF16),
        ),
        in_specs=[VMEM] * 4,
        out_specs=(VMEM,) * 3,
        scratch_shapes=[pltpu.VMEM((8, width), F32)]
        + scatter_scratch(tp_bits, width // 2)
        + gather_scratch(both, width // 2),
        compiler_params=pltpu.CompilerParams(
            collective_id=0, has_side_effects=True, vmem_limit_bytes=need
        ),
    )(values, out_weight, residual, weights)
    return hidden, gathered.reshape(rows, width), weights_all.reshape(rows, 128)


def final(inner, w_down, hidden, groups, peers):
    width = hidden.shape[1]
    grp_bits, tp_bits = axis_bits(groups, peers)
    both = grp_bits + tp_bits
    need = width * 2 * (2 * inner.shape[0] + inner.shape[1]) + (12 << 20)
    return pl.pallas_call(
        functools.partial(final_kernel, both),
        out_shape=jax.ShapeDtypeStruct((8, width), BF16),
        in_specs=[VMEM] * 3,
        out_specs=VMEM,
        scratch_shapes=[pltpu.VMEM((8, width), F32)] + scatter_scratch(both, width // 2),
        compiler_params=pltpu.CompilerParams(
            collective_id=1, has_side_effects=True, vmem_limit_bytes=need
        ),
    )(inner, w_down, hidden)


def body(
    queries,
    kv_cache,
    lengths,
    residual,
    uv_weight,
    out_weight,
    expert_ids,
    gate_values,
    w_gate,
    w_up,
    w_down,
):
    rows_here = residual.shape[0]
    latent = uv_weight.shape[1]
    span = kv_cache.shape[1]
    scores = jnp.einsum(
        "rhc,rlc->rhl", queries, kv_cache, preferred_element_type=jnp.float32
    ) * queries.shape[2] ** (-0.5)
    valid = lax.broadcasted_iota(jnp.int32, (1, 1, span), 2) < lengths[:, None, None]
    top = jnp.max(jnp.where(valid, scores, -jnp.inf), axis=-1, keepdims=True)
    expo = jnp.where(valid, jnp.exp(scores - top), 0.0)
    probs = (expo / jnp.sum(expo, axis=-1, keepdims=True)).astype(jnp.bfloat16)
    context = jnp.einsum(
        "rhl,rlc->rhc", probs, kv_cache[:, :, :latent], preferred_element_type=jnp.float32
    ).astype(jnp.bfloat16)
    groups, peers = lax.axis_size("grp"), lax.axis_size("tp")
    heads_here = uv_weight.shape[0]
    blocks = context.transpose(1, 0, 2).reshape(peers, heads_here * rows_here, latent)
    grouped = exchange(blocks, peers).reshape(peers, heads_here, rows_here, latent)
    values = jnp.einsum(
        "phrc,hcv->prhv", grouped, uv_weight, preferred_element_type=jnp.float32
    ).astype(jnp.bfloat16)
    values = values.reshape(peers * rows_here, heads_here * values.shape[3])
    ids_hot = expert_ids[:, :, None] == lax.broadcasted_iota(jnp.int32, (1, 1, 128), 2)
    weights = jnp.sum(
        jnp.where(ids_hot, gate_values.astype(jnp.float32)[:, :, None], 0.0), axis=1
    )
    hidden_state, rows_all, weights_all = middle(
        values, out_weight, residual, weights, groups, peers
    )
    own = lax.broadcasted_iota(jnp.int32, (1, 128), 1) == lax.axis_index("tp")
    weight = jnp.sum(
        jnp.where(own, weights_all.astype(jnp.float32), 0.0), axis=1, keepdims=True
    )
    gate = jnp.dot(rows_all, w_gate[0], preferred_element_type=jnp.float32)
    up = jnp.dot(rows_all, w_up[0], preferred_element_type=jnp.float32)
    inner = (jax.nn.silu(gate) * up * weight).astype(jnp.bfloat16)
    return final(inner, w_down[0], hidden_state, groups, peers)


def solution(mesh):
    placed = (
        P(("grp", "tp"), None, None),
        P(("grp", "tp"), None, None),
        P(("grp", "tp")),
        P(("grp", "tp"), None),
        P("tp", None, None),
        P("tp", None),
        P(("grp", "tp"), None),
        P(("grp", "tp"), None),
        P("tp", None, "grp"),
        P("tp", None, "grp"),
        P("tp", "grp", None),
    )
    return jax.shard_map(
        body, mesh=mesh, in_specs=placed, out_specs=P(("grp", "tp"), None), check_vma=False
    )
```

```python
import functools
import jax
import jax.numpy as jnp
from jax import lax
from jax.experimental import pallas as pl
from jax.experimental.pallas import tpu as pltpu
from jax.sharding import PartitionSpec as P

TILE = 256
MESH = pl.DeviceIdType.MESH
F32, BF16 = jnp.float32, jnp.bfloat16


def axis_bits(groups, peers):
    grp = [("grp", 1, False)] if groups == 2 else [("grp", 2, True), ("grp", 1, False)]
    tp = [("tp", peers // 2, True), ("tp", peers // 4, False)]
    tp += [("tp", 2, False)] if peers // 8 == 2 else [("tp", 4, True), ("tp", 2, False)]
    return grp, tp


def chain_orders(bits):
    near = [i for i, b in enumerate(bits) if not b[2]]
    far = [i for i, b in enumerate(bits) if b[2]]
    turn = lambda xs, k: xs[k % len(xs):] + xs[: k % len(xs)] if xs else []
    return [turn(near, k) + turn(far, k) for k in range(len(near))]


def column_parts(half, n):
    tiles = half // TILE
    cuts = [TILE * (tiles * k // n) for k in range(n + 1)]
    return [(cuts[k], cuts[k + 1] - cuts[k]) for k in range(n)]


class Place:
    def __init__(self, bits):
        self.g, self.t = lax.axis_index("grp"), lax.axis_index("tp")
        self.core = self.t % 2
        self.sibling = (self.g, self.t + 1 - 2 * self.core)
        self.mine, self.partner = [], []
        for axis, value, _ in bits:
            at = self.g if axis == "grp" else self.t
            bit = (at // value) % 2
            moved = at + value * (1 - 2 * bit)
            self.mine.append(bit)
            self.partner.append((moved, self.t) if axis == "grp" else (self.g, moved))

    def greet(self):
        barrier = pltpu.get_barrier_semaphore()
        others = [self.sibling] + self.partner
        for other in others:
            pl.semaphore_signal(barrier, inc=1, device_id=other, device_id_type=MESH)
        pl.semaphore_wait(barrier, len(others))


def send(src, dst, sems, at, to):
    copy = pltpu.make_async_remote_copy(
        src_ref=src,
        dst_ref=dst,
        send_sem=sems[0].at[at],
        recv_sem=sems[1].at[at],
        device_id=to,
        device_id_type=MESH,
    )
    copy.start()
    return copy


def columns(start, size):
    return pl.ds(pl.multiple_of(start, 128), size)


def scatter_scratch(bits, half):
    shapes = [pltpu.VMEM((2,) * len(bits) + (16, half), BF16), pltpu.VMEM((2, 8, half), F32)]
    shapes += [pltpu.VMEM((8, half), F32), pltpu.VMEM((2,) * len(bits) + (16, half), BF16)]
    orders = chain_orders(bits)
    for _, width in column_parts(half, len(orders)):
        for done in range(len(bits) + 1):
            shapes.append(pltpu.VMEM((2,) * (len(bits) - done) + (16, width), BF16))
    count = len(orders) * (len(bits) + 2)
    return shapes + [pltpu.SemaphoreType.DMA((count,)), pltpu.SemaphoreType.DMA((count,))]


def right_scratch(right, bits):
    count = 2 * len(chain_orders(bits))
    return [pltpu.VMEM(right.shape, right.dtype), pltpu.SemaphoreType.DMA((count,))]


def reduce_scatter(bits, place, half, left_ref, right_ref, right, fetched, out_ref, scratch):
    held, own, swapped, leaving = scratch[:4]
    sems = scratch[-2:]
    orders = chain_orders(bits)
    parts = column_parts(half, len(orders))
    n = len(bits)
    landed = [scratch[4 + k * (n + 1): 4 + (k + 1) * (n + 1)] for k in range(len(orders))]
    every = (slice(None),) * (n + 1)
    core = place.core
    copies, now = [], []

    def launch(*what):
        copy = send(*what)
        copies.append(copy)
        return copy

    loads = []

    def fetch(offset, start, width):
        at = (slice(None), columns(offset + start, width))
        load = pltpu.make_async_copy(right_ref.at[at], right.at[at], fetched.at[len(loads)])
        load.start()
        loads.append(load)

    for start, width in parts:
        fetch((1 - core) * half, start, width)
    for start, width in parts:
        fetch(core * half, start, width)

    def product(offset, start, width, store):
        def tile(i, carry):
            at = pl.multiple_of(start + i * TILE, TILE)
            weight = right[:, columns(offset + at, TILE)]
            value = jnp.dot(left_ref[...], weight, preferred_element_type=F32)
            store(pl.ds(at, TILE), value)
            return carry

        lax.fori_loop(0, width // TILE, tile, 0)

    def leave(here, value):
        leaving[every + (here,)] = value.astype(BF16).reshape(leaving.shape[:-1] + (TILE,))

    def stay(here, value):
        held[every + (here,)] = value.astype(BF16).reshape(held.shape[:-1] + (TILE,))

    for k, (start, width) in enumerate(parts):
        loads[k].wait()
        product((1 - core) * half, start, width, leave)
        src = leaving.at[every + (pl.ds(start, width),)]
        now.append(launch(src, landed[k][0], sems, k * (n + 2), place.sibling))
    for k, (start, width) in enumerate(parts):
        loads[len(parts) + k].wait()
        product(core * half, start, width, stay)
    for stage in range(n + 1):
        for k, (start, width) in enumerate(parts):
            here = pl.ds(start, width)
            now[k].wait_recv()
            done = orders[k][:stage]
            keep = tuple(place.mine[i] if i in done else slice(None) for i in range(n)) + (slice(None),)
            total = held[keep + (here,)].astype(F32) + landed[k][stage][...].astype(F32)
            if stage < n:
                held[keep + (here,)] = total.astype(BF16)
                bit = orders[k][stage]
                away = tuple(
                    1 - place.mine[i] if i == bit else keep[i] for i in range(n)
                ) + (slice(None), here)
                now[k] = launch(
                    held.at[away], landed[k][stage + 1], sems, k * (n + 2) + stage + 1, place.partner[bit]
                )
            else:
                own[0, :, here] = total[:8]
                own[1, :, here] = total[8:]
                now[k] = launch(
                    own.at[1 - core, :, here], swapped.at[:, here], sems, k * (n + 2) + n + 1, place.sibling
                )
    for k, (start, width) in enumerate(parts):
        here = pl.ds(start, width)
        out_ref[:, columns(core * half + start, width)] = own[core, :, here]
        now[k].wait_recv()
        out_ref[:, columns((1 - core) * half + start, width)] = swapped[:, here]
    for copy in copies:
        copy.wait_send()


def gather_scratch(bits, half):
    orders = chain_orders(bits)
    count = (len(orders) + 1) * (len(bits) + 2)
    return [
        pltpu.VMEM((8, half), F32),
        pltpu.VMEM((8, 128), F32),
        pltpu.SemaphoreType.DMA((count,)),
        pltpu.SemaphoreType.DMA((count,)),
    ]


def gather(bits, place, half, rows_ref, small_ref, out_ref, small_out, scratch):
    swapped, small_swapped, sems = scratch[0], scratch[1], scratch[2:]
    orders = chain_orders(bits)
    parts = column_parts(half, len(orders))
    n = len(bits)
    core = place.core
    copies, now = [], []

    def launch(*what):
        copy = send(*what)
        copies.append(copy)
        return copy

    for k, (start, width) in enumerate(parts):
        src = rows_ref.at[:, columns((1 - core) * half + start, width)]
        now.append(launch(src, swapped.at[:, pl.ds(start, width)], sems, k * (n + 2), place.sibling))
    now.append(launch(small_ref, small_swapped, sems, len(parts) * (n + 2), place.sibling))

    def chip_block(mine, other):
        first = jnp.where(core == 0, mine, other)
        second = jnp.where(core == 0, other, mine)
        return jnp.concatenate([first, second], axis=0).astype(BF16)

    own = tuple(place.mine) + (slice(None),)
    for stage in range(n + 1):
        k = len(parts)
        now[k].wait_recv()
        order = orders[0][::-1]
        if stage == 0:
            small_out[own + (slice(None),)] = chip_block(small_ref[...], small_swapped[...])
        if stage < n:
            done = order[:stage]
            at = tuple(slice(None) if i in done else place.mine[i] for i in range(n))
            part = small_out.at[at + (slice(None), slice(None))]
            now[k] = launch(part, part, sems, k * (n + 2) + stage + 1, place.partner[order[stage]])
        for k, (start, width) in enumerate(parts):
            here = columns(core * half + start, width)
            now[k].wait_recv()
            order = orders[k][::-1]
            if stage == 0:
                block = chip_block(rows_ref[:, here], swapped[:, pl.ds(start, width)])
                out_ref[own + (here,)] = block
            done = order[:stage]
            at = tuple(slice(None) if i in done else place.mine[i] for i in range(n))
            part = out_ref.at[at + (slice(None), here)]
            to = place.partner[order[stage]] if stage < n else place.sibling
            now[k] = launch(part, part, sems, k * (n + 2) + stage + 1, to)
    for k in range(len(parts)):
        now[k].wait_recv()
    for copy in copies:
        copy.wait_send()


def middle_kernel(
    tp_bits, all_bits, values_ref, out_weight_ref, residual_ref, weights_ref,
    hidden_ref, rows_ref, weights_out, right, fetched, normed, *scratch
):
    half = residual_ref.shape[1] // 2
    place_all = Place(all_bits)
    place = Place(tp_bits)
    place_all.greet()
    cut = len(scatter_scratch(tp_bits, half))
    reduce_scatter(tp_bits, place, half, values_ref, out_weight_ref, right, fetched, hidden_ref, scratch[:cut])
    state = hidden_ref[...] + residual_ref[...].astype(F32)
    hidden_ref[...] = state
    normed[...] = state * lax.rsqrt(jnp.mean(state * state, axis=-1, keepdims=True) + 1e-06)
    gather(all_bits, place_all, half, normed, weights_ref, rows_ref, weights_out, scratch[cut:])


def final_kernel(all_bits, inner_ref, w_down_ref, hidden_ref, out_ref, right, fetched, routed, *scratch):
    half = hidden_ref.shape[1] // 2
    place = Place(all_bits)
    place.greet()
    reduce_scatter(all_bits, place, half, inner_ref, w_down_ref, right, fetched, routed, scratch)
    out_ref[...] = (routed[...] + hidden_ref[...]).astype(out_ref.dtype)


def exchange_kernel(peers, x_ref, out_ref, send_sems, recv_sems, own_sem):
    g, t = lax.axis_index("grp"), lax.axis_index("tp")
    shifts = sorted(range(1, peers), key=lambda d: (abs(d - peers // 2), d))
    barrier = pltpu.get_barrier_semaphore()
    for d in shifts:
        pl.semaphore_signal(
            barrier, inc=1, device_id=(g, (t + d) % peers), device_id_type=MESH
        )
    pl.semaphore_wait(barrier, peers - 1)
    copies = []
    for d in shifts:
        to = (t + d) % peers
        copies.append(send(x_ref.at[to], out_ref.at[t], (send_sems, recv_sems), d, (g, to)))
    own = pltpu.make_async_copy(x_ref.at[t], out_ref.at[t], own_sem)
    own.start()
    own.wait()
    for copy in copies:
        copy.wait_recv()
    for copy in copies:
        copy.wait_send()


VMEM = pl.BlockSpec(memory_space=pltpu.VMEM)
ANY = pl.BlockSpec(memory_space=pl.ANY)


def exchange(blocks, peers):
    return pl.pallas_call(
        functools.partial(exchange_kernel, peers),
        out_shape=jax.ShapeDtypeStruct(blocks.shape, blocks.dtype),
        in_specs=[VMEM],
        out_specs=VMEM,
        scratch_shapes=[
            pltpu.SemaphoreType.DMA((peers,)),
            pltpu.SemaphoreType.DMA((peers,)),
            pltpu.SemaphoreType.DMA(()),
        ],
        compiler_params=pltpu.CompilerParams(
            collective_id=2, has_side_effects=True, vmem_limit_bytes=8 << 20
        ),
    )(blocks)


def middle(values, out_weight, residual, weights, groups, peers):
    width = residual.shape[1]
    grp_bits, tp_bits = axis_bits(groups, peers)
    both = grp_bits + tp_bits
    rows = groups * peers * 8
    need = width * 2 * (3 * values.shape[0] + rows + values.shape[1]) + (12 << 20)
    shape = (2,) * len(both) + (16,)
    hidden, gathered, weights_all = pl.pallas_call(
        functools.partial(middle_kernel, tp_bits, both),
        out_shape=(
            jax.ShapeDtypeStruct((8, width), F32),
            jax.ShapeDtypeStruct(shape + (width,), BF16),
            jax.ShapeDtypeStruct(shape + (128,), BF16),
        ),
        in_specs=[VMEM, ANY, VMEM, VMEM],
        out_specs=(VMEM,) * 3,
        scratch_shapes=right_scratch(out_weight, tp_bits)
        + [pltpu.VMEM((8, width), F32)]
        + scatter_scratch(tp_bits, width // 2)
        + gather_scratch(both, width // 2),
        compiler_params=pltpu.CompilerParams(
            collective_id=0, has_side_effects=True, vmem_limit_bytes=need
        ),
    )(values, out_weight, residual, weights)
    return hidden, gathered.reshape(rows, width), weights_all.reshape(rows, 128)


def final(inner, w_down, hidden, groups, peers):
    width = hidden.shape[1]
    grp_bits, tp_bits = axis_bits(groups, peers)
    both = grp_bits + tp_bits
    need = width * 2 * (2 * inner.shape[0] + inner.shape[1]) + (12 << 20)
    return pl.pallas_call(
        functools.partial(final_kernel, both),
        out_shape=jax.ShapeDtypeStruct((8, width), BF16),
        in_specs=[VMEM, ANY, VMEM],
        out_specs=VMEM,
        scratch_shapes=right_scratch(w_down, both)
        + [pltpu.VMEM((8, width), F32)]
        + scatter_scratch(both, width // 2),
        compiler_params=pltpu.CompilerParams(
            collective_id=1, has_side_effects=True, vmem_limit_bytes=need
        ),
    )(inner, w_down, hidden)


def body(
    queries,
    kv_cache,
    lengths,
    residual,
    uv_weight,
    out_weight,
    expert_ids,
    gate_values,
    w_gate,
    w_up,
    w_down,
):
    rows_here = residual.shape[0]
    latent = uv_weight.shape[1]
    span = kv_cache.shape[1]
    scores = jnp.einsum(
        "rhc,rlc->rhl", queries, kv_cache, preferred_element_type=jnp.float32
    ) * queries.shape[2] ** (-0.5)
    valid = lax.broadcasted_iota(jnp.int32, (1, 1, span), 2) < lengths[:, None, None]
    top = jnp.max(jnp.where(valid, scores, -jnp.inf), axis=-1, keepdims=True)
    expo = jnp.where(valid, jnp.exp(scores - top), 0.0)
    probs = (expo / jnp.sum(expo, axis=-1, keepdims=True)).astype(jnp.bfloat16)
    context = jnp.einsum(
        "rhl,rlc->rhc", probs, kv_cache[:, :, :latent], preferred_element_type=jnp.float32
    ).astype(jnp.bfloat16)
    groups, peers = lax.axis_size("grp"), lax.axis_size("tp")
    heads_here = uv_weight.shape[0]
    blocks = context.transpose(1, 0, 2).reshape(peers, heads_here * rows_here, latent)
    grouped = exchange(blocks, peers).reshape(peers, heads_here, rows_here, latent)
    values = jnp.einsum(
        "phrc,hcv->prhv", grouped, uv_weight, preferred_element_type=jnp.float32
    ).astype(jnp.bfloat16)
    values = values.reshape(peers * rows_here, heads_here * values.shape[3])
    ids_hot = expert_ids[:, :, None] == lax.broadcasted_iota(jnp.int32, (1, 1, 128), 2)
    weights = jnp.sum(
        jnp.where(ids_hot, gate_values.astype(jnp.float32)[:, :, None], 0.0), axis=1
    )
    hidden_state, rows_all, weights_all = middle(
        values, out_weight, residual, weights, groups, peers
    )
    own = lax.broadcasted_iota(jnp.int32, (1, 128), 1) == lax.axis_index("tp")
    weight = jnp.sum(
        jnp.where(own, weights_all.astype(jnp.float32), 0.0), axis=1, keepdims=True
    )
    gate = jnp.dot(rows_all, w_gate[0], preferred_element_type=jnp.float32)
    up = jnp.dot(rows_all, w_up[0], preferred_element_type=jnp.float32)
    inner = (jax.nn.silu(gate) * up * weight).astype(jnp.bfloat16)
    return final(inner, w_down[0], hidden_state, groups, peers)


def solution(mesh):
    placed = (
        P(("grp", "tp"), None, None),
        P(("grp", "tp"), None, None),
        P(("grp", "tp")),
        P(("grp", "tp"), None),
        P("tp", None, None),
        P("tp", None),
        P(("grp", "tp"), None),
        P(("grp", "tp"), None),
        P("tp", None, "grp"),
        P("tp", None, "grp"),
        P("tp", "grp", None),
    )
    return jax.shard_map(
        body, mesh=mesh, in_specs=placed, out_specs=P(("grp", "tp"), None), check_vma=False
    )
```
